32 devices in a mesh: win: 2 (over y), tile: 4 (over z), sec: 4 (over x, core).
Axes of the slice: x: 2, y: 2, z: 4, core: 2. Of those that a mesh axis runs over, the one named last changes fastest.
Arguments:
- step_field: float32 [64, 2, 32, 256], P(('win', 'sec'), None, 'tile'), parts along dimension 0, may hold values from -4 to 4
- offsets: int32 [64, 2, 2, 32, 256], P(('win', 'sec'), None, None, 'tile'), parts along dimension 0, may hold values from -4 to 4
- fraction: float32 [64, 2, 2, 32, 256], P(('win', 'sec'), None, None, 'tile'), parts along dimension 0, may hold values from 0 to 1
- flow_mask: int32 [64, 2, 32, 256], P(('win', 'sec'), None, 'tile'), parts along dimension 0, may hold values 0 or 1
Outputs:
- displacement: float32 [64, 2, 32, 256], P(('win', 'sec'), None, 'tile'), parts along dimension 0
The draws below stay inside these ranges and needn't reach their ends.
There are 2 independent parts, one for each index of `win`. The reference program is written for one: setup_inputs(seed, part) draws one part's arguments, and reference() takes and returns one part's arrays. A program takes and returns all parts, laid end to end along the dimension named above; each array names one. Nothing has to cross between parts.
All inputs are finite; a program needn't handle non-finite values. No bound on the sum of `flow_mask` on one device may be relied on, other than what follows from the above.
Results may differ from the reference program's by a relative error of at most 0.00002.
Values sent between devices are 32-bit elements; how exact they have to be, the bound alone decides.
A program may use at most 64 MiB of HBM per device.

```python
import jax
import jax.numpy as jnp

NX = 256
REACH = 4
ITERS = 4
NY = 32
SECTIONS = 32


def place_ends(array, rng, low, high):
    shape = array.shape
    index_at = [jax.random.randint(jax.random.fold_in(rng, axis), (), 0, shape[axis]) for axis in range(len(shape))]
    array = array.at[tuple(index_at)].set(low)
    longest = shape.index(max(shape))
    index_at[longest] = (index_at[longest] + 1) % shape[longest]
    return array.at[tuple(index_at)].set(high)


def steps_of(rng, shape, cuts, least, high):
    def one(position, shards_of):
        steps = jax.random.uniform(jax.random.fold_in(jax.random.fold_in(rng, 6), position), (shards_of,), jnp.float32, least / len(cuts), high / len(cuts))
        return jnp.repeat(jnp.exp(steps), shape[position] // shards_of).reshape((-1,) + (1,) * (len(shape) - position - 1))

    gain = one(*cuts[0])
    for cut in cuts[1:]:
        gain = gain * one(*cut)
    return gain


def bell_draw(own_key, shape, spread, limit, pieces=(), held_as=jnp.bfloat16):
    result = spread * jax.random.normal(own_key, shape, jnp.float32)
    if pieces:
        result = result * steps_of(own_key, shape, pieces, -0.22, 0.18)
    return jnp.clip(result, -limit, limit).astype(held_as)


def setup_inputs(seed: int = 0, part: int = 0) -> dict:
    seeds = jax.random.split(jax.random.key(seed), 5)
    own_keys = jax.random.split(jax.random.fold_in(seeds[4], part), 5)
    return {
        "step_field": bell_draw(own_keys[0], (SECTIONS, 2, NY, NX), 0.5, 4.0, ((0, 4), (2, 4)), jnp.float32),
        "offsets": place_ends(jax.random.randint(own_keys[1], (SECTIONS, 2, 2, NY, NX), 0 - REACH, REACH + 1), jax.random.fold_in(own_keys[1], 1), 0 - REACH, REACH).astype(jnp.int32),
        "fraction": jnp.clip(1.0 * jax.random.uniform(own_keys[2], (SECTIONS, 2, 2, NY, NX), jnp.float32) ** steps_of(own_keys[2], (SECTIONS, 2, 2, NY, NX), ((0, 4), (3, 4)), -0.2, 0.2), 0.0, 1.0),
        "flow_mask": place_ends((jax.random.randint(own_keys[3], (SECTIONS, 2, NY, NX), 0, 8) < 7).astype(jnp.int32), jax.random.fold_in(own_keys[3], 1), 0, 1),
    }


STEP = 0.25
STIFF_PLANE = 1.0
STIFF_CROSS = 1.0


def interpolate(source, row_off, col_off, row_frac, col_frac, extent):
    margin = extent + 1
    count = row_off.shape[0]
    row_total = row_off.shape[1]
    col_total = row_off.shape[2]
    summed = jnp.zeros((count, 2, row_total, col_total), jnp.float32)
    for shift_row in range(-extent, extent + 2):
        row_weight = jnp.where(row_off == shift_row, 1.0 - row_frac, 0.0) + jnp.where(row_off + 1 == shift_row, row_frac, 0.0)
        stripe = source[:, :, margin + shift_row: margin + shift_row + row_total, :]
        partial_sum = jnp.zeros((count, 2, row_total, col_total), jnp.float32)
        for shift_col in range(-extent, extent + 2):
            col_weight = jnp.where(col_off == shift_col, 1.0 - col_frac, 0.0) + jnp.where(col_off + 1 == shift_col, col_frac, 0.0)
            partial_sum = partial_sum + col_weight[:, None] * stripe[:, :, :, margin + shift_col: margin + shift_col + col_total]
        summed = summed + row_weight[:, None] * partial_sum
    return summed


def node_forces(own, below, above, offsets, fraction, flow_mask, first_row, first_sec, total_rows, total_secs, extent):
    margin = extent + 1
    count = offsets.shape[0]
    row_total = offsets.shape[3]
    col_total = offsets.shape[4]
    center = own[:, :, margin:margin + row_total, margin:margin + col_total]
    global_row = (jnp.arange(row_total, dtype=jnp.int32) + first_row)[:, None]
    column = jnp.arange(col_total, dtype=jnp.int32)[None, :]
    upper = own[:, :, margin - 1:margin - 1 + row_total, margin:margin + col_total]
    lower = own[:, :, margin + 1:margin + 1 + row_total, margin:margin + col_total]
    left = own[:, :, margin:margin + row_total, margin - 1:margin - 1 + col_total]
    right = own[:, :, margin:margin + row_total, margin + 1:margin + 1 + col_total]
    plane = jnp.where(global_row >= 1, upper - center, 0.0)
    plane = plane + jnp.where(global_row <= total_rows - 2, lower - center, 0.0)
    plane = plane + jnp.where(column >= 1, left - center, 0.0)
    plane = plane + jnp.where(column <= col_total - 2, right - center, 0.0)
    section = jnp.arange(count, dtype=jnp.int32) + first_sec
    cross = jnp.zeros_like(center)
    sources = (below, above)
    for side in range(2):
        row_off = offsets[:, side, 0]
        col_off = offsets[:, side, 1]
        row_frac = fraction[:, side, 0]
        col_frac = fraction[:, side, 1]
        target_row = global_row[None] + row_off
        target_col = column[None] + col_off
        if side == 0:
            section_live = section >= 1
        else:
            section_live = section <= total_secs - 2
        live = (target_row >= 0) & (target_row <= total_rows - 2) & (target_col >= 0) & (target_col <= col_total - 2)
        live = live & (flow_mask[:, side] == 1) & section_live[:, None, None]
        sampled = interpolate(sources[side], row_off, col_off, row_frac, col_frac, extent)
        flow = jnp.stack([row_off.astype(jnp.float32) + row_frac, col_off.astype(jnp.float32) + col_frac], axis=1)
        cross = cross + jnp.where(live[:, None], sampled + flow - center, 0.0)
    return STIFF_PLANE * plane + STIFF_CROSS * cross


def reference(step_field, offsets, fraction, flow_mask):
    field = jnp.cumsum(step_field, axis=0)
    margin = REACH + 1
    for sweep in range(ITERS):
        padded = jnp.pad(field, ((0, 0), (0, 0), (margin, margin), (margin, margin)))
        zeroed = jnp.zeros_like(padded[:1])
        below = jnp.concatenate([zeroed, padded[:-1]], axis=0)
        above = jnp.concatenate([padded[1:], zeroed], axis=0)
        field = field + STEP * node_forces(padded, below, above, offsets, fraction, flow_mask, 0, 0, NY, SECTIONS, REACH)
    return field
```

```python
import functools

import jax
import jax.numpy as jnp
from jax import lax
from jax.experimental import pallas as pl
from jax.experimental.pallas import tpu as pltpu
from jax.sharding import PartitionSpec as P

REACH = 4
ITERS = 4
STEP = 0.25
ROWS = 8
LANES = 128
SHIFTS = 2 * REACH + 2
MESH = pl.DeviceIdType.MESH
DIRECTIONS = ((0, 1), (0, -1), (1, 1), (1, -1), (-1, 1), (-1, -1), (1, 0), (-1, 0))


def lane_ids():
    return lax.broadcasted_iota(jnp.int32, (ROWS, LANES), 1)


def middle_of(a0, b0, a1, b1):
    lane = lax.broadcasted_iota(jnp.int32, a0.shape, 1)
    first = pltpu.roll(jnp.where(lane >= 64, a0, b0), 32, 1)
    second = pltpu.roll(jnp.where(lane >= 64, a1, b1), 96, 1)
    return jnp.where(lane < 64, first, second)


def pick(values, index):
    return jnp.take_along_axis(values, index, axis=1, mode="promise_in_bounds")


def kernel(
    n_tile, n_sec, step_ref, off_ref, frac_ref, mask_ref, out_ref,
    field, totals, base, index0, index1, col_frac, row_weight, flow_sum, degree,
    send_sem, recv_sem, total_send, total_recv,
):
    count = step_ref.shape[0]
    tile = lax.axis_index("tile")
    sec = lax.axis_index("sec")

    def there(dt, ds):
        ok = None
        for here, d, n in ((tile, dt, n_tile), (sec, ds, n_sec)):
            if d:
                test = here + d < n if d > 0 else here + d >= 0
                ok = test if ok is None else jnp.logical_and(ok, test)
        return ok

    @pl.when(tile == 0)
    def _():
        field[:, :, :, 0:ROWS, :] = jnp.zeros((ITERS, count + 2, 5, ROWS, LANES), jnp.float32)

    @pl.when(tile == n_tile - 1)
    def _():
        field[:, :, :, 2 * ROWS:, :] = jnp.zeros((ITERS, count + 2, 5, ROWS, LANES), jnp.float32)

    @pl.when(sec == 0)
    def _():
        field[:, 0] = jnp.zeros((ITERS, 5, 3 * ROWS, LANES), jnp.float32)

    @pl.when(sec == n_sec - 1)
    def _():
        field[:, count + 1] = jnp.zeros((ITERS, 5, 3 * ROWS, LANES), jnp.float32)

    barrier = pltpu.get_barrier_semaphore()

    def greet(peer):
        pl.semaphore_signal(barrier, inc=1, device_id=peer, device_id_type=MESH)

    for dt, ds in DIRECTIONS:
        if dt:

            @pl.when(there(dt, ds))
            def _():
                greet({"tile": tile + dt, "sec": sec + ds})

    for other in range(n_sec):

        @pl.when(sec != other)
        def _():
            greet({"sec": other})

    def beside(here, n):
        return jnp.where(here > 0, 1, 0) + jnp.where(here < n - 1, 1, 0)

    pl.semaphore_wait(barrier, n_sec - 1 + beside(tile, n_tile) * (1 + beside(sec, n_sec)))

    for c in range(2):
        for h in range(2):
            k = 2 * c + h
            running = step_ref[0, c, :, h * LANES:(h + 1) * LANES]
            field[0, 1, k, ROWS:2 * ROWS, :] = running
            for s in range(1, count):
                running = running + step_ref[s, c, :, h * LANES:(h + 1) * LANES]
                field[0, s + 1, k, ROWS:2 * ROWS, :] = running
            base[k] = running

    def total_copy(source, target):
        return pltpu.make_async_remote_copy(
            src_ref=base, dst_ref=totals.at[source], send_sem=total_send.at[target],
            recv_sem=total_recv.at[source], device_id={"sec": target}, device_id_type=MESH,
        )

    for source in range(n_sec - 1):

        @pl.when(sec == source)
        def _():
            for target in range(source + 1, n_sec):
                total_copy(source, target).start()

    lane = lane_ids()
    row = lax.broadcasted_iota(jnp.int32, (ROWS, LANES), 0) + tile * ROWS
    last_row = n_tile * ROWS - 1
    last_col = 2 * LANES - 1

    def prepare(s, carry):
        flows = [[jnp.zeros((ROWS, LANES), jnp.float32) for _ in range(2)] for _ in range(2)]
        live_count = []
        for h in range(2):
            column = lane + h * LANES
            four = jnp.where(row >= 1, 1.0, 0.0) + jnp.where(row <= last_row - 1, 1.0, 0.0)
            four = four + jnp.where(column >= 1, 1.0, 0.0) + jnp.where(column <= last_col - 1, 1.0, 0.0)
            live_count.append(four)
        for side in range(2):
            j = 2 * s + side
            if side == 0:
                section_live = jnp.logical_or(sec > 0, s >= 1)
            else:
                section_live = jnp.logical_or(sec < n_sec - 1, s <= count - 2)
            halves = []
            for h in range(2):
                part = slice(h * LANES, (h + 1) * LANES)
                ro, co = off_ref[s, side, 0, :, part], off_ref[s, side, 1, :, part]
                rf, cf = frac_ref[s, side, 0, :, part], frac_ref[s, side, 1, :, part]
                target_row, target_col = row + ro, lane + h * LANES + co
                live = (target_row >= 0) & (target_row <= last_row - 1)
                live = live & (target_col >= 0) & (target_col <= last_col - 1)
                live = live & (mask_ref[s, side, :, part] == 1)
                gain = jnp.where(section_live, 1.0, 0.0)
                live = jnp.where(live, 1.0, 0.0) * gain
                flows[0][h] = flows[0][h] + live * (ro.astype(jnp.float32) + rf)
                flows[1][h] = flows[1][h] + live * (co.astype(jnp.float32) + cf)
                live_count[h] = live_count[h] + live
                halves.append((ro, co, live * (1.0 - rf), live * rf, cf))
            a, b = halves
            halves.append(tuple(middle_of(x, y, x, y) for x, y in zip(a, b)))
            for t, (ro, co, low, high, cf) in enumerate(halves):
                index0[j, t] = jnp.clip(lane + co, 0, LANES - 1)
                index1[j, t] = jnp.clip(lane + co + 1, 0, LANES - 1)
                col_frac[j, t] = cf
                for d in range(SHIFTS):
                    shift = d - REACH
                    row_weight[j, t, d] = jnp.where(ro == shift, low, jnp.where(ro == shift - 1, high, 0.0))
        for h in range(2):
            degree[s, h] = live_count[h]
            for c in range(2):
                flow_sum[s, 2 * c + h] = flows[c][h]
        return carry

    lax.fori_loop(0, count, prepare, 0)

    for source in range(n_sec - 1):

        @pl.when(sec > source)
        def _():
            total_copy(source, source + 1).wait_recv()

        @pl.when(sec == source)
        def _():
            for target in range(source + 1, n_sec):
                total_copy(source, target).wait_send()

    base[...] = jnp.zeros(base.shape, jnp.float32)
    for source in range(n_sec - 1):

        @pl.when(sec > source)
        def _():
            base[...] = base[...] + totals[source]

    for s in range(count):
        for k in range(4):
            field[0, s + 1, k, ROWS:2 * ROWS, :] = field[0, s + 1, k, ROWS:2 * ROWS, :] + base[k]

    def halo_copy(sweep, number):
        dt, ds = DIRECTIONS[number]
        if ds == 0:
            source = target = pl.ds(1, count)
        elif ds > 0:
            source, target = pl.ds(count, 1), pl.ds(0, 1)
        else:
            source, target = pl.ds(1, 1), pl.ds(count + 1, 1)
        landing = pl.ds({1: 0, 0: ROWS, -1: 2 * ROWS}[dt], ROWS)
        peer = {}
        if dt:
            peer["tile"] = tile + dt
        if ds:
            peer["sec"] = sec + ds
        return pltpu.make_async_remote_copy(
            src_ref=field.at[sweep, source, pl.ds(0, 4), pl.ds(ROWS, ROWS)],
            dst_ref=field.at[sweep, target, pl.ds(0, 4), landing],
            send_sem=send_sem.at[sweep, number], recv_sem=recv_sem.at[sweep, number],
            device_id=peer, device_id_type=MESH,
        )

    for sweep in range(ITERS):
        for number, (dt, ds) in enumerate(DIRECTIONS):

            @pl.when(there(dt, ds))
            def _():
                halo_copy(sweep, number).start()

        for number, (dt, ds) in enumerate(DIRECTIONS):

            @pl.when(there(-dt, -ds))
            def _():
                halo_copy(sweep, number).wait_recv()

        def middle(slot, carry):
            parts = [field[sweep, slot, k] for k in range(4)]
            field[sweep, slot, 4] = middle_of(*parts)
            return carry

        lax.fori_loop(0, count + 2, middle, 0)

        def relax(s, carry):
            sums = [None] * 5
            for side in range(2):
                j = 2 * s + side
                slot = s + 2 * side
                i0 = [index0[j, t] for t in range(3)]
                i1 = [index1[j, t] for t in range(3)]
                cf = [col_frac[j, t] for t in range(3)]
                for d in range(SHIFTS):
                    top = ROWS - REACH + d
                    weight = [row_weight[j, t, d] for t in range(3)]
                    for k in range(5):
                        t = 2 if k == 4 else k % 2
                        source = field[sweep, slot, k, top:top + ROWS, :]
                        low, high = pick(source, i0[t]), pick(source, i1[t])
                        term = weight[t] * (low + cf[t] * (high - low))
                        sums[k] = term if sums[k] is None else sums[k] + term
            for c in range(2):
                seam = pltpu.roll(sums[4], 96 if c == 0 else 32, 1)
                cross = (
                    jnp.where(lane < 112, sums[2 * c], seam),
                    jnp.where(lane < 16, seam, sums[2 * c + 1]),
                )
                own = [field[sweep, s + 1, 2 * c + h, ROWS:2 * ROWS, :] for h in range(2)]
                left = [pltpu.roll(x, 1, 1) for x in own]
                right = [pltpu.roll(x, LANES - 1, 1) for x in own]
                sides = (
                    jnp.where(lane == 0, 0.0, left[0]) + jnp.where(lane == LANES - 1, right[1], right[0]),
                    jnp.where(lane == 0, left[0], left[1]) + jnp.where(lane == LANES - 1, 0.0, right[1]),
                )
                for h in range(2):
                    k = 2 * c + h
                    above = field[sweep, s + 1, k, ROWS - 1:2 * ROWS - 1, :]
                    below = field[sweep, s + 1, k, ROWS + 1:2 * ROWS + 1, :]
                    force = cross[h] + flow_sum[s, k] + sides[h] + (above + below) - degree[s, h] * own[h]
                    new = own[h] + STEP * force
                    if sweep == ITERS - 1:
                        out_ref[s, c, :, h * LANES:(h + 1) * LANES] = new
                    else:
                        field[sweep + 1, s + 1, k, ROWS:2 * ROWS, :] = new
            return carry

        lax.fori_loop(0, count, relax, 0)

    for sweep in range(ITERS):
        for number, (dt, ds) in enumerate(DIRECTIONS):

            @pl.when(there(dt, ds))
            def _():
                halo_copy(sweep, number).wait_send()


def per_device(n_tile, n_sec, step_field, offsets, fraction, flow_mask):
    count = step_field.shape[0]
    vmem = pl.BlockSpec(memory_space=pltpu.VMEM)
    f32, i32 = jnp.float32, jnp.int32
    return pl.pallas_call(
        functools.partial(kernel, n_tile, n_sec),
        out_shape=jax.ShapeDtypeStruct(step_field.shape, f32),
        in_specs=[vmem] * 4,
        out_specs=vmem,
        scratch_shapes=[
            pltpu.VMEM((ITERS, count + 2, 5, 3 * ROWS, LANES), f32),
            pltpu.VMEM((n_sec, 4, ROWS, LANES), f32),
            pltpu.VMEM((4, ROWS, LANES), f32),
            pltpu.VMEM((2 * count, 3, ROWS, LANES), i32),
            pltpu.VMEM((2 * count, 3, ROWS, LANES), i32),
            pltpu.VMEM((2 * count, 3, ROWS, LANES), f32),
            pltpu.VMEM((2 * count, 3, SHIFTS, ROWS, LANES), f32),
            pltpu.VMEM((count, 4, ROWS, LANES), f32),
            pltpu.VMEM((count, 2, ROWS, LANES), f32),
            pltpu.SemaphoreType.DMA((ITERS, len(DIRECTIONS))),
            pltpu.SemaphoreType.DMA((ITERS, len(DIRECTIONS))),
            pltpu.SemaphoreType.DMA((n_sec,)),
            pltpu.SemaphoreType.DMA((n_sec,)),
        ],
        compiler_params=pltpu.CompilerParams(
            collective_id=0, has_side_effects=True, vmem_limit_bytes=32 * 1024 * 1024
        ),
    )(step_field, offsets, fraction, flow_mask)


def solution(mesh):
    spec = P(("win", "sec"), None, "tile", None)
    flow_spec = P(("win", "sec"), None, None, "tile", None)
    return jax.shard_map(
        functools.partial(per_device, mesh.shape["tile"], mesh.shape["sec"]),
        mesh=mesh,
        in_specs=(spec, flow_spec, flow_spec, spec),
        out_specs=spec,
        check_vma=False,
    )
```

```python
import functools

import jax
import jax.numpy as jnp
from jax import lax
from jax.experimental import pallas as pl
from jax.experimental.pallas import tpu as pltpu
from jax.sharding import PartitionSpec as P

REACH = 4
ITERS = 4
STEP = 0.25
ROWS = 8
UP = REACH
DOWN = REACH + 1
LANES = 128
SHIFTS = 2 * REACH + 2
MESH = pl.DeviceIdType.MESH
DIRECTIONS = ((0, 1), (0, -1), (1, 1), (1, -1), (-1, 1), (-1, -1), (1, 0), (-1, 0))


def middle_of(a0, b0, a1, b1):
    lane = lax.broadcasted_iota(jnp.int32, a0.shape, 1)
    first = pltpu.roll(jnp.where(lane >= 64, a0, b0), 32, 1)
    second = pltpu.roll(jnp.where(lane >= 64, a1, b1), 96, 1)
    return jnp.where(lane < 64, first, second)


def pick(values, index):
    return jnp.take_along_axis(values, index, axis=1, mode="promise_in_bounds")


def kernel(
    n_tile, n_sec, step_ref, off_ref, frac_ref, mask_ref, out_ref,
    field, outer, edge, source, partial, turned, totals, base,
    index0, index1, col_frac, row_weight, flow_sum, degree,
    send_sem, recv_sem, total_send, total_recv,
):
    count = step_ref.shape[0]
    block = (count, LANES)
    f32 = jnp.float32
    tile = lax.axis_index("tile")
    sec = lax.axis_index("sec")
    span = UP + ROWS + DOWN
    halves = [slice(h * LANES, (h + 1) * LANES) for h in range(2)]

    def there(dt, ds):
        ok = None
        for here, d, n in ((tile, dt, n_tile), (sec, ds, n_sec)):
            if d:
                test = here + d < n if d > 0 else here + d >= 0
                ok = test if ok is None else jnp.logical_and(ok, test)
        return ok

    def clear(test, *places):
        @pl.when(test)
        def _():
            for ref in places:
                ref[...] = jnp.zeros(ref.shape, f32)

    clear(tile == 0, field.at[pl.ds(0, ITERS), pl.ds(0, UP)], edge.at[:, :, pl.ds(0, UP)])
    clear(tile == n_tile - 1, field.at[pl.ds(0, ITERS), pl.ds(UP + ROWS, DOWN)], edge.at[:, :, pl.ds(UP + ROWS, DOWN)])
    clear(sec == 0, edge.at[:, 0])
    clear(sec == n_sec - 1, edge.at[:, 1])

    barrier = pltpu.get_barrier_semaphore()

    def greet(peer):
        pl.semaphore_signal(barrier, inc=1, device_id=peer, device_id_type=MESH)

    for dt, ds in DIRECTIONS:
        if dt:

            @pl.when(there(dt, ds))
            def _():
                greet({"tile": tile + dt, "sec": sec + ds})

    for other in range(n_sec):

        @pl.when(sec != other)
        def _():
            greet({"sec": other})

    def beside(here, n):
        return jnp.where(here > 0, 1, 0) + jnp.where(here < n - 1, 1, 0)

    for c in range(2):
        for h in range(2):
            running = step_ref[0, c, :, halves[h]]
            turned[2 * c + h, 0] = running
            for s in range(1, count):
                running = running + step_ref[s, c, :, halves[h]]
                turned[2 * c + h, s] = running
            base[2 * c + h] = running

    pl.semaphore_wait(barrier, n_sec - 1 + beside(tile, n_tile) * (1 + beside(sec, n_sec)))

    def total_copy(origin, target):
        return pltpu.make_async_remote_copy(
            src_ref=base, dst_ref=totals.at[origin], send_sem=total_send.at[target],
            recv_sem=total_recv.at[origin], device_id={"sec": target}, device_id_type=MESH,
        )

    for origin in range(n_sec - 1):

        @pl.when(sec == origin)
        def _():
            for target in range(origin + 1, n_sec):
                total_copy(origin, target).start()

    for side in range(2):
        for h in range(2):
            for n, ref in enumerate((off_ref, frac_ref)):
                for c in range(2):
                    item = 8 * n + 4 * side + 2 * c + h
                    flipped = jnp.swapaxes(ref[:, side, c, :, halves[h]].astype(f32), 0, 1)
                    turned[4 + item] = flipped
            turned[20 + 2 * side + h] = jnp.swapaxes(mask_ref[:, side, :, halves[h]].astype(f32), 0, 1)

    lane = lax.broadcasted_iota(jnp.int32, block, 1)
    sub = lax.broadcasted_iota(jnp.int32, block, 0)
    section = sub + sec * count
    last_row = n_tile * ROWS - 1
    last_col = 2 * LANES - 1

    def prepare(r, carry):
        row = r + tile * ROWS
        flows = [[jnp.zeros(block, f32) for _ in range(2)] for _ in range(2)]
        live_count = []
        for h in range(2):
            column = lane + h * LANES
            four = jnp.where(row + 0 * column >= 1, 1.0, 0.0) + jnp.where(row + 0 * column <= last_row - 1, 1.0, 0.0)
            four = four + jnp.where(column >= 1, 1.0, 0.0) + jnp.where(column <= last_col - 1, 1.0, 0.0)
            live_count.append(four)
        for side in range(2):
            section_live = section >= 1 if side == 0 else section <= n_sec * count - 2
            parts = []
            for h in range(2):
                ro, co = (turned[4 + 4 * side + 2 * c + h, r].astype(jnp.int32) for c in range(2))
                rf, cf = (turned[12 + 4 * side + 2 * c + h, r] for c in range(2))
                target_row, target_col = row + ro, lane + h * LANES + co
                live = (target_row >= 0) & (target_row <= last_row - 1)
                live = live & (target_col >= 0) & (target_col <= last_col - 1)
                live = live & (turned[20 + 2 * side + h, r] == 1.0) & section_live
                live = jnp.where(live, 1.0, 0.0)
                flows[0][h] = flows[0][h] + live * (ro.astype(f32) + rf)
                flows[1][h] = flows[1][h] + live * (co.astype(f32) + cf)
                live_count[h] = live_count[h] + live
                parts.append((ro, co, live * (1.0 - rf), live * rf, cf))
            a, b = parts
            parts.append(tuple(middle_of(x, y, x, y) for x, y in zip(a, b)))
            for t, (ro, co, low, high, cf) in enumerate(parts):
                index0[r, side, t] = jnp.clip(lane + co, 0, LANES - 1)
                index1[r, side, t] = jnp.clip(lane + co + 1, 0, LANES - 1)
                col_frac[r, side, t] = cf
                for d in range(SHIFTS):
                    shift = d - REACH
                    row_weight[r, side, t, d] = jnp.where(ro == shift, low, jnp.where(ro == shift - 1, high, 0.0))
        for h in range(2):
            degree[r, h] = live_count[h]
            for c in range(2):
                flow_sum[r, 2 * c + h] = flows[c][h]
        return carry

    lax.fori_loop(0, ROWS, prepare, 0)

    for origin in range(n_sec - 1):

        @pl.when(sec > origin)
        def _():
            total_copy(origin, origin + 1).wait_recv()

        @pl.when(sec == origin)
        def _():
            for target in range(origin + 1, n_sec):
                total_copy(origin, target).wait_send()

    base[...] = jnp.zeros(base.shape, f32)
    for origin in range(n_sec - 1):

        @pl.when(sec > origin)
        def _():
            base[...] = base[...] + totals[origin]

    for k in range(4):
        field[0, UP:UP + ROWS, k] = jnp.swapaxes(turned[k] + base[k][None], 0, 1)

    sent_rows = {1: pl.ds(UP + ROWS - UP, UP), 0: pl.ds(UP, ROWS), -1: pl.ds(UP, DOWN)}
    landing_rows = {1: pl.ds(0, UP), 0: pl.ds(UP, ROWS), -1: pl.ds(UP + ROWS, DOWN)}

    def halo_copy(sweep, number):
        dt, ds = DIRECTIONS[number]
        if ds == 0:
            src, dst = field.at[sweep, sent_rows[dt]], field.at[sweep, landing_rows[dt]]
        else:
            which = 0 if ds > 0 else 1
            src, dst = outer.at[sweep, which, sent_rows[dt]], edge.at[sweep, which, landing_rows[dt]]
        peer = {}
        if dt:
            peer["tile"] = tile + dt
        if ds:
            peer["sec"] = sec + ds
        return pltpu.make_async_remote_copy(
            src_ref=src, dst_ref=dst,
            send_sem=send_sem.at[sweep, number], recv_sem=recv_sem.at[sweep, number],
            device_id=peer, device_id_type=MESH,
        )

    def arrive(sweep, diagonal_or_tile):
        for number, (dt, ds) in enumerate(DIRECTIONS):
            if (dt != 0) == diagonal_or_tile:

                @pl.when(there(-dt, -ds))
                def _():
                    halo_copy(sweep, number).wait_recv()

    def make_sources(sweep, rows):
        for q in rows:
            below, above = [], []
            for k in range(4):
                own = field[sweep, q, k]
                under = jnp.broadcast_to(edge[sweep, 0, q, k:k + 1, :], block)
                over = jnp.broadcast_to(edge[sweep, 1, q, k:k + 1, :], block)
                below.append(jnp.where(sub == 0, under, pltpu.roll(own, 1, 0)))
                above.append(jnp.where(sub == count - 1, over, pltpu.roll(own, count - 1, 0)))
            for side, parts in enumerate((below, above)):
                parts.append(middle_of(*parts))
                for k in range(5):
                    source[side, q, k] = parts[k]

    def gather_rows(r, wanted, sums):
        for side in range(2):
            i0 = [index0[r, side, t] for t in range(3)]
            i1 = [index1[r, side, t] for t in range(3)]
            cf = [col_frac[r, side, t] for t in range(3)]
            for d in range(SHIFTS):
                if not wanted(r + d):
                    continue
                weight = [row_weight[r, side, t, d] for t in range(3)]
                for k in range(5):
                    t = 2 if k == 4 else k % 2
                    values = source[side, r + d, k]
                    low, high = pick(values, i0[t]), pick(values, i1[t])
                    term = weight[t] * (low + cf[t] * (high - low))
                    sums[k] = term if sums[k] is None else sums[k] + term
        return sums

    def is_own(q):
        return UP <= q < UP + ROWS

    def relax(sweep, carry):
        for q in range(UP, UP + ROWS):
            for k in range(4):
                outer[sweep, 0, q, k:k + 1, :] = field[sweep, q, k, count - 1:count, :]
                outer[sweep, 1, q, k:k + 1, :] = field[sweep, q, k, 0:1, :]
        for number, (dt, ds) in enumerate(DIRECTIONS):

            @pl.when(there(dt, ds))
            def _():
                halo_copy(sweep, number).start()

        arrive(sweep, False)
        make_sources(sweep, range(UP, UP + ROWS))
        for r in range(ROWS):
            sums = gather_rows(r, is_own, [None] * 5)
            for k in range(5):
                partial[r, k] = sums[k]
        arrive(sweep, True)
        make_sources(sweep, [q for q in range(span) if not is_own(q)])
        for r in range(ROWS):
            sums = gather_rows(r, lambda q: not is_own(q), [partial[r, k] for k in range(5)])
            for c in range(2):
                seam = pltpu.roll(sums[4], 96 if c == 0 else 32, 1)
                cross = (
                    jnp.where(lane < 112, sums[2 * c], seam),
                    jnp.where(lane < 16, seam, sums[2 * c + 1]),
                )
                own = [field[sweep, UP + r, 2 * c + h] for h in range(2)]
                left = [pltpu.roll(x, 1, 1) for x in own]
                right = [pltpu.roll(x, LANES - 1, 1) for x in own]
                sides = (
                    jnp.where(lane == 0, 0.0, left[0]) + jnp.where(lane == LANES - 1, right[1], right[0]),
                    jnp.where(lane == 0, left[0], left[1]) + jnp.where(lane == LANES - 1, 0.0, right[1]),
                )
                for h in range(2):
                    k = 2 * c + h
                    above, below = field[sweep, UP + r - 1, k], field[sweep, UP + r + 1, k]
                    force = cross[h] + flow_sum[r, k] + sides[h] + (above + below) - degree[r, h] * own[h]
                    field[sweep + 1, UP + r, k] = own[h] + STEP * force
        for number, (dt, ds) in enumerate(DIRECTIONS):

            @pl.when(there(dt, ds))
            def _():
                halo_copy(sweep, number).wait_send()

        return carry

    lax.fori_loop(0, ITERS, relax, 0)
    for c in range(2):
        for h in range(2):
            out_ref[:, c, :, halves[h]] = jnp.swapaxes(field[ITERS, UP:UP + ROWS, 2 * c + h], 0, 1)


def per_device(n_tile, n_sec, step_field, offsets, fraction, flow_mask):
    count = step_field.shape[0]
    span = UP + ROWS + DOWN
    vmem = pl.BlockSpec(memory_space=pltpu.VMEM)
    f32, i32 = jnp.float32, jnp.int32
    return pl.pallas_call(
        functools.partial(kernel, n_tile, n_sec),
        out_shape=jax.ShapeDtypeStruct(step_field.shape, f32),
        in_specs=[vmem] * 4,
        out_specs=vmem,
        scratch_shapes=[
            pltpu.VMEM((ITERS + 1, span, 4, count, LANES), f32),
            pltpu.VMEM((ITERS, 2, span, 4, LANES), f32),
            pltpu.VMEM((ITERS, 2, span, 4, LANES), f32),
            pltpu.VMEM((2, span, 5, count, LANES), f32),
            pltpu.VMEM((ROWS, 5, count, LANES), f32),
            pltpu.VMEM((24, count, ROWS, LANES), f32),
            pltpu.VMEM((n_sec, 4, ROWS, LANES), f32),
            pltpu.VMEM((4, ROWS, LANES), f32),
            pltpu.VMEM((ROWS, 2, 3, count, LANES), i32),
            pltpu.VMEM((ROWS, 2, 3, count, LANES), i32),
            pltpu.VMEM((ROWS, 2, 3, count, LANES), f32),
            pltpu.VMEM((ROWS, 2, 3, SHIFTS, count, LANES), f32),
            pltpu.VMEM((ROWS, 4, count, LANES), f32),
            pltpu.VMEM((ROWS, 2, count, LANES), f32),
            pltpu.SemaphoreType.DMA((ITERS, len(DIRECTIONS))),
            pltpu.SemaphoreType.DMA((ITERS, len(DIRECTIONS))),
            pltpu.SemaphoreType.DMA((n_sec,)),
            pltpu.SemaphoreType.DMA((n_sec,)),
        ],
        compiler_params=pltpu.CompilerParams(
            collective_id=0, has_side_effects=True, vmem_limit_bytes=32 * 1024 * 1024
        ),
    )(step_field, offsets, fraction, flow_mask)


def solution(mesh):
    spec = P(("win", "sec"), None, "tile", None)
    flow_spec = P(("win", "sec"), None, None, "tile", None)
    return jax.shard_map(
        functools.partial(per_device, mesh.shape["tile"], mesh.shape["sec"]),
        mesh=mesh,
        in_specs=(spec, flow_spec, flow_spec, spec),
        out_specs=spec,
        check_vma=False,
    )
```

```python
import functools

import jax
import jax.numpy as jnp
from jax import lax
from jax.experimental import pallas as pl
from jax.experimental.pallas import tpu as pltpu
from jax.sharding import PartitionSpec as P

REACH = 4
ITERS = 4
STEP = 0.25
ROWS = 8
UP = REACH
DOWN = REACH + 1
LANES = 128
SHIFTS = 2 * REACH + 2
MESH = pl.DeviceIdType.MESH
DIRECTIONS = ((0, 1), (0, -1), (1, 1), (1, -1), (-1, 1), (-1, -1), (1, 0), (-1, 0))


def middle_of(a0, b0, a1, b1):
    lane = lax.broadcasted_iota(jnp.int32, a0.shape, 1)
    first = pltpu.roll(jnp.where(lane >= 64, a0, b0), 32, 1)
    second = pltpu.roll(jnp.where(lane >= 64, a1, b1), 96, 1)
    return jnp.where(lane < 64, first, second)


def pick(values, index):
    return jnp.take_along_axis(values, index, axis=1, mode="promise_in_bounds")


def kernel(
    n_tile, n_sec, step_hbm, off_hbm, frac_hbm, mask_hbm, out_ref,
    step_ref, off_ref, frac_ref, mask_ref, load_sem, field, outer, edge, source, partial, turned, totals, base,
    index0, index1, col_frac, row_weight, flow_sum, degree,
    send_sem, recv_sem, total_send, total_recv,
):
    loads = [
        pltpu.make_async_copy(far, near, load_sem.at[i])
        for i, (far, near) in enumerate(
            ((step_hbm, step_ref), (off_hbm, off_ref), (frac_hbm, frac_ref), (mask_hbm, mask_ref))
        )
    ]
    for load in loads:
        load.start()
    count = step_ref.shape[0]
    block = (count, LANES)
    f32 = jnp.float32
    tile = lax.axis_index("tile")
    sec = lax.axis_index("sec")
    span = UP + ROWS + DOWN
    halves = [slice(h * LANES, (h + 1) * LANES) for h in range(2)]

    def there(dt, ds):
        ok = None
        for here, d, n in ((tile, dt, n_tile), (sec, ds, n_sec)):
            if d:
                test = here + d < n if d > 0 else here + d >= 0
                ok = test if ok is None else jnp.logical_and(ok, test)
        return ok

    def clear(test, *places):
        @pl.when(test)
        def _():
            for ref in places:
                ref[...] = jnp.zeros(ref.shape, f32)

    clear(tile == 0, field.at[pl.ds(0, ITERS), pl.ds(0, UP)], edge.at[:, :, pl.ds(0, UP)])
    clear(tile == n_tile - 1, field.at[pl.ds(0, ITERS), pl.ds(UP + ROWS, DOWN)], edge.at[:, :, pl.ds(UP + ROWS, DOWN)])
    clear(sec == 0, edge.at[:, 0])
    clear(sec == n_sec - 1, edge.at[:, 1])

    barrier = pltpu.get_barrier_semaphore()

    def greet(peer):
        pl.semaphore_signal(barrier, inc=1, device_id=peer, device_id_type=MESH)

    for dt, ds in DIRECTIONS:
        if dt:

            @pl.when(there(dt, ds))
            def _():
                greet({"tile": tile + dt, "sec": sec + ds})

    for other in range(n_sec):

        @pl.when(sec != other)
        def _():
            greet({"sec": other})

    def beside(here, n):
        return jnp.where(here > 0, 1, 0) + jnp.where(here < n - 1, 1, 0)

    loads[0].wait()
    for c in range(2):
        for h in range(2):
            running = step_ref[0, c, :, halves[h]]
            turned[2 * c + h, 0] = running
            for s in range(1, count):
                running = running + step_ref[s, c, :, halves[h]]
                turned[2 * c + h, s] = running
            base[2 * c + h] = running

    pl.semaphore_wait(barrier, n_sec - 1 + beside(tile, n_tile) * (1 + beside(sec, n_sec)))

    def total_copy(origin, target):
        return pltpu.make_async_remote_copy(
            src_ref=base, dst_ref=totals.at[origin], send_sem=total_send.at[target],
            recv_sem=total_recv.at[origin], device_id={"sec": target}, device_id_type=MESH,
        )

    for origin in range(n_sec - 1):

        @pl.when(sec == origin)
        def _():
            for target in range(origin + 1, n_sec):
                total_copy(origin, target).start()

    for load in loads[1:]:
        load.wait()
    for side in range(2):
        for h in range(2):
            for n, ref in enumerate((off_ref, frac_ref)):
                for c in range(2):
                    item = 8 * n + 4 * side + 2 * c + h
                    flipped = jnp.swapaxes(ref[:, side, c, :, halves[h]].astype(f32), 0, 1)
                    turned[4 + item] = flipped
            turned[20 + 2 * side + h] = jnp.swapaxes(mask_ref[:, side, :, halves[h]].astype(f32), 0, 1)

    lane = lax.broadcasted_iota(jnp.int32, block, 1)
    sub = lax.broadcasted_iota(jnp.int32, block, 0)
    section = sub + sec * count
    last_row = n_tile * ROWS - 1
    last_col = 2 * LANES - 1

    def prepare(r, carry):
        row = r + tile * ROWS
        flows = [[jnp.zeros(block, f32) for _ in range(2)] for _ in range(2)]
        live_count = []
        for h in range(2):
            column = lane + h * LANES
            four = jnp.where(row + 0 * column >= 1, 1.0, 0.0) + jnp.where(row + 0 * column <= last_row - 1, 1.0, 0.0)
            four = four + jnp.where(column >= 1, 1.0, 0.0) + jnp.where(column <= last_col - 1, 1.0, 0.0)
            live_count.append(four)
        for side in range(2):
            section_live = section >= 1 if side == 0 else section <= n_sec * count - 2
            parts = []
            for h in range(2):
                ro, co = (turned[4 + 4 * side + 2 * c + h, r].astype(jnp.int32) for c in range(2))
                rf, cf = (turned[12 + 4 * side + 2 * c + h, r] for c in range(2))
                target_row, target_col = row + ro, lane + h * LANES + co
                live = (target_row >= 0) & (target_row <= last_row - 1)
                live = live & (target_col >= 0) & (target_col <= last_col - 1)
                live = live & (turned[20 + 2 * side + h, r] == 1.0) & section_live
                live = jnp.where(live, 1.0, 0.0)
                flows[0][h] = flows[0][h] + live * (ro.astype(f32) + rf)
                flows[1][h] = flows[1][h] + live * (co.astype(f32) + cf)
                live_count[h] = live_count[h] + live
                parts.append((ro, co, live * (1.0 - rf), live * rf, cf))
            a, b = parts
            parts.append(tuple(middle_of(x, y, x, y) for x, y in zip(a, b)))
            for t, (ro, co, low, high, cf) in enumerate(parts):
                index0[r, side, t] = jnp.clip(lane + co, 0, LANES - 1)
                index1[r, side, t] = jnp.clip(lane + co + 1, 0, LANES - 1)
                col_frac[r, side, t] = cf
                for d in range(SHIFTS):
                    shift = d - REACH
                    row_weight[r, side, t, d] = jnp.where(ro == shift, low, jnp.where(ro == shift - 1, high, 0.0))
        for h in range(2):
            degree[r, h] = live_count[h]
            for c in range(2):
                flow_sum[r, 2 * c + h] = flows[c][h]
        return carry

    lax.fori_loop(0, ROWS, prepare, 0)

    for origin in range(n_sec - 1):

        @pl.when(sec > origin)
        def _():
            total_copy(origin, origin + 1).wait_recv()

        @pl.when(sec == origin)
        def _():
            for target in range(origin + 1, n_sec):
                total_copy(origin, target).wait_send()

    base[...] = jnp.zeros(base.shape, f32)
    for origin in range(n_sec - 1):

        @pl.when(sec > origin)
        def _():
            base[...] = base[...] + totals[origin]

    for k in range(4):
        field[0, UP:UP + ROWS, k] = jnp.swapaxes(turned[k] + base[k][None], 0, 1)

    sent_rows = {1: pl.ds(UP + ROWS - UP, UP), 0: pl.ds(UP, ROWS), -1: pl.ds(UP, DOWN)}
    landing_rows = {1: pl.ds(0, UP), 0: pl.ds(UP, ROWS), -1: pl.ds(UP + ROWS, DOWN)}

    def halo_copy(sweep, number):
        dt, ds = DIRECTIONS[number]
        if ds == 0:
            src, dst = field.at[sweep, sent_rows[dt]], field.at[sweep, landing_rows[dt]]
        else:
            which = 0 if ds > 0 else 1
            src, dst = outer.at[sweep, which, sent_rows[dt]], edge.at[sweep, which, landing_rows[dt]]
        peer = {}
        if dt:
            peer["tile"] = tile + dt
        if ds:
            peer["sec"] = sec + ds
        return pltpu.make_async_remote_copy(
            src_ref=src, dst_ref=dst,
            send_sem=send_sem.at[sweep, number], recv_sem=recv_sem.at[sweep, number],
            device_id=peer, device_id_type=MESH,
        )

    def arrive(sweep, diagonal_or_tile):
        for number, (dt, ds) in enumerate(DIRECTIONS):
            if (dt != 0) == diagonal_or_tile:

                @pl.when(there(-dt, -ds))
                def _():
                    halo_copy(sweep, number).wait_recv()

    def make_sources(sweep, rows):
        for q in rows:
            below, above = [], []
            for k in range(4):
                own = field[sweep, q, k]
                under = jnp.broadcast_to(edge[sweep, 0, q, k:k + 1, :], block)
                over = jnp.broadcast_to(edge[sweep, 1, q, k:k + 1, :], block)
                below.append(jnp.where(sub == 0, under, pltpu.roll(own, 1, 0)))
                above.append(jnp.where(sub == count - 1, over, pltpu.roll(own, count - 1, 0)))
            for side, parts in enumerate((below, above)):
                parts.append(middle_of(*parts))
                for k in range(5):
                    source[side, q, k] = parts[k]

    def gather_rows(r, wanted, sums):
        for side in range(2):
            i0 = [index0[r, side, t] for t in range(3)]
            i1 = [index1[r, side, t] for t in range(3)]
            cf = [col_frac[r, side, t] for t in range(3)]
            for d in range(SHIFTS):
                if not wanted(r + d):
                    continue
                weight = [row_weight[r, side, t, d] for t in range(3)]
                for k in range(5):
                    t = 2 if k == 4 else k % 2
                    values = source[side, r + d, k]
                    low, high = pick(values, i0[t]), pick(values, i1[t])
                    term = weight[t] * (low + cf[t] * (high - low))
                    sums[k] = term if sums[k] is None else sums[k] + term
        return sums

    def is_own(q):
        return UP <= q < UP + ROWS

    def send(sweep, rows, wanted):
        for q in rows:
            for k in range(4):
                outer[sweep, 0, q, k:k + 1, :] = field[sweep, q, k, count - 1:count, :]
                outer[sweep, 1, q, k:k + 1, :] = field[sweep, q, k, 0:1, :]
        for number, (dt, ds) in enumerate(DIRECTIONS):
            if wanted(dt):

                @pl.when(there(dt, ds))
                def _():
                    halo_copy(sweep, number).start()

    def relax(sweep, carry):
        arrive(sweep, False)
        make_sources(sweep, range(UP, UP + ROWS))
        for r in range(ROWS):
            sums = gather_rows(r, is_own, [None] * 5)
            for k in range(5):
                partial[r, k] = sums[k]
        arrive(sweep, True)
        make_sources(sweep, [q for q in range(span) if not is_own(q)])
        for r in range(ROWS):
            sums = gather_rows(r, lambda q: not is_own(q), [partial[r, k] for k in range(5)])
            for c in range(2):
                seam = pltpu.roll(sums[4], 96 if c == 0 else 32, 1)
                cross = (
                    jnp.where(lane < 112, sums[2 * c], seam),
                    jnp.where(lane < 16, seam, sums[2 * c + 1]),
                )
                own = [field[sweep, UP + r, 2 * c + h] for h in range(2)]
                left = [pltpu.roll(x, 1, 1) for x in own]
                right = [pltpu.roll(x, LANES - 1, 1) for x in own]
                sides = (
                    jnp.where(lane == 0, 0.0, left[0]) + jnp.where(lane == LANES - 1, right[1], right[0]),
                    jnp.where(lane == 0, left[0], left[1]) + jnp.where(lane == LANES - 1, 0.0, right[1]),
                )
                for h in range(2):
                    k = 2 * c + h
                    above, below = field[sweep, UP + r - 1, k], field[sweep, UP + r + 1, k]
                    force = cross[h] + flow_sum[r, k] + sides[h] + (above + below) - degree[r, h] * own[h]
                    field[sweep + 1, UP + r, k] = own[h] + STEP * force
            if r == DOWN - 1:

                @pl.when(sweep < ITERS - 1)
                def _():
                    send(sweep + 1, range(UP, UP + DOWN), lambda dt: dt < 0)

        @pl.when(sweep < ITERS - 1)
        def _():
            send(sweep + 1, range(UP + DOWN, UP + ROWS), lambda dt: dt >= 0)

        return carry

    send(0, range(UP, UP + ROWS), lambda dt: True)
    lax.fori_loop(0, ITERS, relax, 0)
    for sweep in range(ITERS):
        for number, (dt, ds) in enumerate(DIRECTIONS):

            @pl.when(there(dt, ds))
            def _():
                halo_copy(sweep, number).wait_send()

    for c in range(2):
        for h in range(2):
            out_ref[:, c, :, halves[h]] = jnp.swapaxes(field[ITERS, UP:UP + ROWS, 2 * c + h], 0, 1)


def per_device(n_tile, n_sec, step_field, offsets, fraction, flow_mask):
    count = step_field.shape[0]
    span = UP + ROWS + DOWN
    vmem = pl.BlockSpec(memory_space=pltpu.VMEM)
    f32, i32 = jnp.float32, jnp.int32
    return pl.pallas_call(
        functools.partial(kernel, n_tile, n_sec),
        out_shape=jax.ShapeDtypeStruct(step_field.shape, f32),
        in_specs=[pl.BlockSpec(memory_space=pl.ANY)] * 4,
        out_specs=vmem,
        scratch_shapes=[
            pltpu.VMEM(step_field.shape, f32),
            pltpu.VMEM(offsets.shape, i32),
            pltpu.VMEM(fraction.shape, f32),
            pltpu.VMEM(flow_mask.shape, i32),
            pltpu.SemaphoreType.DMA((4,)),
            pltpu.VMEM((ITERS + 1, span, 4, count, LANES), f32),
            pltpu.VMEM((ITERS, 2, span, 4, LANES), f32),
            pltpu.VMEM((ITERS, 2, span, 4, LANES), f32),
            pltpu.VMEM((2, span, 5, count, LANES), f32),
            pltpu.VMEM((ROWS, 5, count, LANES), f32),
            pltpu.VMEM((24, count, ROWS, LANES), f32),
            pltpu.VMEM((n_sec, 4, ROWS, LANES), f32),
            pltpu.VMEM((4, ROWS, LANES), f32),
            pltpu.VMEM((ROWS, 2, 3, count, LANES), i32),
            pltpu.VMEM((ROWS, 2, 3, count, LANES), i32),
            pltpu.VMEM((ROWS, 2, 3, count, LANES), f32),
            pltpu.VMEM((ROWS, 2, 3, SHIFTS, count, LANES), f32),
            pltpu.VMEM((ROWS, 4, count, LANES), f32),
            pltpu.VMEM((ROWS, 2, count, LANES), f32),
            pltpu.SemaphoreType.DMA((ITERS, len(DIRECTIONS))),
            pltpu.SemaphoreType.DMA((ITERS, len(DIRECTIONS))),
            pltpu.SemaphoreType.DMA((n_sec,)),
            pltpu.SemaphoreType.DMA((n_sec,)),
        ],
        compiler_params=pltpu.CompilerParams(
            collective_id=0, has_side_effects=True, vmem_limit_bytes=60 * 1024 * 1024
        ),
    )(step_field, offsets, fraction, flow_mask)


def solution(mesh):
    spec = P(("win", "sec"), None, "tile", None)
    flow_spec = P(("win", "sec"), None, None, "tile", None)
    return jax.shard_map(
        functools.partial(per_device, mesh.shape["tile"], mesh.shape["sec"]),
        mesh=mesh,
        in_specs=(spec, flow_spec, flow_spec, spec),
        out_specs=spec,
        check_vma=False,
    )
```
